128 devices in a mesh: depth: 16 (over x, z_lo, core), group: 8 (over z_hi, y).
Axes of the slice: x: 4, y: 4, z: 4 (z_hi: 2, z_lo: 2; z = z_hi * 2 + z_lo), core: 2. Of those that a mesh axis runs over, the one named last changes fastest.
Arguments:
- output_one: bfloat16 [32, 256, 128, 128], P(None, 'depth', 'group'), may hold values from -6 to 6
- output_two: bfloat16 [32, 256, 128, 128], P(None, 'depth', 'group'), may hold values from -6 to 6
- cotangent_one: bfloat16 [32, 256, 128, 128], P(None, 'depth', 'group'), may hold values from -6 to 6
- cotangent_two: bfloat16 [32, 256, 128, 128], P(None, 'depth', 'group'), may hold values from -6 to 6
- first_weight: bfloat16 [27, 32, 32], replicated, may hold values from -0.21875 to 0.21875
- second_weight: bfloat16 [27, 32, 32], replicated, may hold values from -0.21875 to 0.21875
- bricks: int32 [16, 8, 8], P('depth'), may hold values from 0 to 8, as said below
Outputs:
- restored_one: bfloat16 [32, 256, 128, 128], P(None, 'depth', 'group')
- restored_two: bfloat16 [32, 256, 128, 128], P(None, 'depth', 'group')
- input_grad_one: bfloat16 [32, 256, 128, 128], P(None, 'depth', 'group')
- input_grad_two: bfloat16 [32, 256, 128, 128], P(None, 'depth', 'group')
- first_weight_grad: float32 [27, 32, 32], replicated
- second_weight_grad: float32 [27, 32, 32], replicated
The draws below stay inside these ranges and needn't reach their ends.
Inputs may be any that keep to these rules, and one draw needn't show every extreme that they name: bricks[z, g, :] lists the positions of the occupied bricks of depth layer z and lateral row g, distinct and ascending, followed by 8 in every unused entry. For each z the numbers of occupied bricks over g = 0 .. 7 are a reordering of 1 + (7 * j * j) // 49 for j = 0 .. 7, so in every depth layer one row has all 8 bricks occupied and the layer holds at most 32 occupied bricks.
All inputs are finite; a program needn't handle non-finite values.
Results may differ from the reference program's by a relative error of at most 0.0085.
Values may be sent and summed in bfloat16 or wider, within the bound.
A program may use at most 256 MiB of HBM per device.

```python
import math
import jax
import jax.numpy as jnp
from jax import lax

CH = 32
B = 16
BX = 8
NBZ = 16
NBY = 8
NZ = 256
NY = 128
NX = 128


def draw_bricks(key, part):
    count_key = jax.random.fold_in(key, 101)
    order_key = jax.random.fold_in(key, 202)
    indices = jnp.arange(NBY, dtype=jnp.int32)
    pattern = 1 + (BX - 1) * indices * indices // ((NBY - 1) * (NBY - 1))
    row_keys = jax.random.split(count_key, NBZ)
    counts = jax.vmap(lambda row_key: jax.random.permutation(row_key, pattern))(row_keys)
    scores = jax.random.randint(order_key, (NBZ, NBY, BX), 0, 1 << 20) * BX + jnp.arange(BX, dtype=jnp.int32)
    shuffled = jnp.argsort(scores, axis=-1).astype(jnp.int32)
    chosen = jnp.where(jnp.arange(BX, dtype=jnp.int32)[None, None, :] < counts[:, :, None], shuffled, BX)
    return jnp.sort(chosen, axis=-1).astype(jnp.int32)


def block_levels(stream_key, shape, cuts, least, high):
    factor_of = 1.0
    for axis_at, blocks in cuts:
        steps = jax.random.uniform(jax.random.fold_in(jax.random.fold_in(stream_key, 6), axis_at), (blocks,), jnp.float32, least / len(cuts), high / len(cuts))
        factor_of = factor_of * jnp.repeat(jnp.exp(steps), shape[axis_at] // blocks).reshape((-1,) + (1,) * (len(shape) - 1 - axis_at))
    return factor_of


def noise(own_key, shape, scale, bound, cuts=(), kind=jnp.bfloat16):
    entries = jax.random.normal(own_key, shape, jnp.float32) * scale
    if len(cuts) > 0:
        entries = block_levels(own_key, shape, cuts, -0.22, 0.18) * entries
    return jnp.clip(entries, min=-bound, max=bound).astype(kind)


def setup_inputs(seed: int = 0) -> dict:
    arg_keys = jax.random.split(jax.random.key(seed), 8)
    return {
        "output_one": noise(arg_keys[0], (CH, NZ, NY, NX), 1.0, 6.0, ((1, 16), (2, 8))),
        "output_two": noise(arg_keys[1], (CH, NZ, NY, NX), 1.0, 6.0, ((1, 16), (2, 8))),
        "cotangent_one": noise(arg_keys[2], (CH, NZ, NY, NX), 1.0, 6.0, ((1, 16), (2, 8))),
        "cotangent_two": noise(arg_keys[3], (CH, NZ, NY, NX), 1.0, 6.0, ((1, 16), (2, 8))),
        "first_weight": noise(arg_keys[4], (27, CH, CH), (27 * CH) ** -0.5, 0.21875),
        "second_weight": noise(arg_keys[5], (27, CH, CH), (27 * CH) ** -0.5, 0.21875),
        "bricks": draw_bricks(jax.random.fold_in(arg_keys[7], 71), 0),
    }


def logistic_slope(inputs):
    logistic = jax.nn.sigmoid(inputs)
    return logistic * (1.0 + inputs * (1.0 - logistic))

def correlate(window, kernel):
    channels_out = kernel.shape[1]
    channels_in = kernel.shape[2]
    shaped_kernel = jnp.transpose(kernel.reshape(3, 3, 3, channels_out, channels_in), (3, 4, 0, 1, 2))
    result = lax.conv_general_dilated(window[None], shaped_kernel, (1, 1, 1), 'VALID', dimension_numbers=('NCDHW', 'OIDHW', 'NCDHW'), precision=lax.Precision.HIGHEST)
    return result[0]

def flipped(kernel):
    return jnp.transpose(jnp.flip(kernel, 0), (0, 2, 1))

def tap_slices(window, brick_edge):
    pieces = []
    for depth_step in range(3):
        for row_step in range(3):
            for col_step in range(3):
                pieces.append(window[:, depth_step:depth_step + brick_edge, row_step:row_step + brick_edge, col_step:col_step + brick_edge])
    return jnp.stack(pieces, axis=0)

def weight_gradient(errors, window, brick_edge):
    return jnp.einsum('ozyx,tizyx->toi', errors, tap_slices(window, brick_edge), precision=lax.Precision.HIGHEST)

def reference(output_one, output_two, cotangent_one, cotangent_two, first_weight, second_weight, bricks):
    window_edge = B + 2
    slots_total = NBZ * NBY * BX
    present = jnp.any(bricks[:, :, :, None] == jnp.arange(BX, dtype=jnp.int32)[None, None, None, :], axis=2)
    present = present.astype(jnp.float32)
    voxel_mask = jnp.repeat(jnp.repeat(jnp.repeat(present, B, axis=0), B, axis=1), B, axis=2)
    first_kernel = first_weight.astype(jnp.float32)
    second_kernel = second_weight.astype(jnp.float32)

    def padded_volume(volume):
        return jnp.pad(volume, ((0, 0), (1, 1), (1, 1), (1, 1)))

    def locate(number):
        depth_index = (number // (NBY * BX)).astype(jnp.int32)
        row_index = (number // BX % NBY).astype(jnp.int32)
        col_index = (number % BX).astype(jnp.int32)
        return (depth_index, row_index, col_index)

    def cut(volume, corner, extent):
        start = (jnp.zeros((), jnp.int32),) + corner
        return lax.dynamic_slice(volume, start, (volume.shape[0], extent, extent, extent)).astype(jnp.float32)

    def place(volume, brick, corner):
        start = (jnp.zeros((), jnp.int32),) + corner
        return lax.dynamic_update_slice(volume, brick.astype(volume.dtype), start)

    def sweep(work, carry):

        def visit(number, state):
            depth_index, row_index, col_index = locate(number)
            corner = ((depth_index * B).astype(jnp.int32), (row_index * B).astype(jnp.int32), (col_index * B).astype(jnp.int32))
            return lax.cond(present[depth_index, row_index, col_index] > 0, lambda inner: work(inner, corner), lambda inner: inner, state)
        return lax.fori_loop(0, slots_total, visit, carry)
    zero_volume = jnp.zeros(output_one.shape, jnp.bfloat16)
    zero_grad = jnp.zeros(second_weight.shape, jnp.float32)
    upper_masked = (output_one.astype(jnp.float32) * voxel_mask).astype(jnp.bfloat16)
    padded_upper = padded_volume(upper_masked)

    def first_work(state, corner):
        shaped, errors, partials = state
        window = cut(padded_upper, corner, window_edge)
        preact = correlate(window, second_kernel)
        cotangent_brick = cut(cotangent_two, corner, B)
        shaped_brick = jax.nn.silu(preact).astype(jnp.bfloat16)
        error_brick = (cotangent_brick * logistic_slope(preact)).astype(jnp.bfloat16)
        partials = partials + weight_gradient(error_brick.astype(jnp.float32), window, B)
        return (place(shaped, shaped_brick, corner), place(errors, error_brick, corner), partials)
    shaped_g, errors_g, second_grad = sweep(first_work, (zero_volume, zero_volume, zero_grad))
    restored_two = (output_two.astype(jnp.float32) - shaped_g.astype(jnp.float32)).astype(jnp.bfloat16)
    lower_masked = (restored_two.astype(jnp.float32) * voxel_mask).astype(jnp.bfloat16)
    padded_lower = padded_volume(lower_masked)
    padded_errors = padded_volume(errors_g)
    second_back = flipped(second_kernel)

    def second_work(state, corner):
        totals, shaped, errors, partials = state
        window = cut(padded_lower, corner, window_edge)
        preact = correlate(window, first_kernel)
        spread = correlate(cut(padded_errors, corner, window_edge), second_back)
        total_brick = (cut(cotangent_one, corner, B) + spread).astype(jnp.bfloat16)
        shaped_brick = jax.nn.silu(preact).astype(jnp.bfloat16)
        error_brick = (total_brick.astype(jnp.float32) * logistic_slope(preact)).astype(jnp.bfloat16)
        partials = partials + weight_gradient(error_brick.astype(jnp.float32), window, B)
        return (place(totals, total_brick, corner), place(shaped, shaped_brick, corner), place(errors, error_brick, corner), partials)
    input_grad_one, shaped_f, errors_f, first_grad = sweep(second_work, (cotangent_one, zero_volume, zero_volume, zero_grad))
    restored_one = (output_one.astype(jnp.float32) - shaped_f.astype(jnp.float32)).astype(jnp.bfloat16)
    padded_last = padded_volume(errors_f)
    first_back = flipped(first_kernel)

    def third_work(state, corner):
        spread = correlate(cut(padded_last, corner, window_edge), first_back)
        return place(state, (cut(cotangent_two, corner, B) + spread).astype(jnp.bfloat16), corner)
    input_grad_two = sweep(third_work, cotangent_two)
    scale = 1.0 / math.sqrt(float(NZ * NY * NX))
    return (restored_one, restored_two, input_grad_one, input_grad_two, first_grad * scale, second_grad * scale)
```

```python
import math

import jax
import jax.numpy as jnp
from jax import lax
from jax.experimental import pallas as pl
from jax.experimental.pallas import tpu as pltpu
from jax.sharding import PartitionSpec as P

MESH = pl.DeviceIdType.MESH
BF = jnp.bfloat16
F32 = jnp.float32

CH = 32
B = 16
NX = 128
ND = 16
NG = 8
CHUNKS = 12
DIRS = tuple((dz, dy) for dz in (-1, 0, 1) for dy in (-1, 0, 1) if (dz, dy) != (0, 0))


def dot(a, b):
    return lax.dot_general(a, b, (((1,), (0,)), ((), ())), preferred_element_type=F32)


def dot_nt(a, b):
    return lax.dot_general(a, b, (((1,), (1,)), ((), ())), preferred_element_type=F32)


def permutation():
    row = lax.broadcasted_iota(jnp.int32, (256, 256), 0)
    col = lax.broadcasted_iota(jnp.int32, (256, 256), 1)
    return jnp.where((row & 15) * 16 + (row >> 4) == col, 1.0, 0.0).astype(BF)


def lane():
    return lax.broadcasted_iota(jnp.int32, (1, NX), 1)


def shift_up(values):
    return jnp.where(lane() == 0, 0.0, pltpu.roll(values, 1, 1))


def shift_down(values):
    return jnp.where(lane() == NX - 1, 0.0, pltpu.roll(values, NX - 1, 1))


def band_rows(blocks, out_ref):
    zeros = jnp.zeros((CH, NX), F32)
    for c in range(3):
        wide = jnp.concatenate([blocks(a, c) for a in range(3)] + [zeros], axis=1)
        for zo in range(2):
            for yo in range(2):
                turn = (zo * 4 + yo) * CH
                moved = wide if turn == 0 else pltpu.roll(wide, turn, 1)
                row = (c * 4 + zo * 2 + yo) * CH
                out_ref[row : row + CH, :] = moved.astype(BF)


def build_band(w_ref, out_ref):
    def blocks(a, c):
        taps = [w_ref[9 * a + 3 * b + c].astype(F32) for b in range(3)]
        return jnp.concatenate(taps + [jnp.zeros((CH, CH), F32)], axis=1)

    band_rows(blocks, out_ref)


def build_band_transposed(w_ref, out_ref):
    def blocks(a, c):
        taps = [w_ref[26 - (9 * a + 3 * b + c)].astype(F32) for b in range(3)]
        tall = jnp.concatenate(taps + [jnp.zeros((CH, CH), F32)], axis=0)
        square = jnp.concatenate([tall, jnp.zeros((NX, NX - CH), F32)], axis=1)
        return jnp.transpose(square)[:CH]

    band_rows(blocks, out_ref)


def fused(
    o1, o2, c1, c2, w1_ref, w2_ref, bricks_ref,
    r1_out, r2_out, g1_out, g2_out, t1_out, t2_out,
    n_o1, n_o2, n_c1, n_c2,
    q_o1, q_o2, q_c1, q_c2,
    p_u, p_l, p_eg, p_ef,
    shifted, perm, band_f, band_g, band_tf, band_tg, acc,
    part, rs_in, ar_in, tot,
    in_sem, out_sem, hs, hr, rs_s, rs_r, ar_s, ar_r, ag_s, ag_r,
):
    depth = lax.axis_index("depth")
    group = lax.axis_index("group")

    def exists(dz, dy):
        ok = None
        for d, at, size in ((dz, depth, ND), (dy, group, NG)):
            if d == 0:
                continue
            here = at > 0 if d < 0 else at < size - 1
            ok = here if ok is None else jnp.logical_and(ok, here)
        return ok

    def clamp(dz, dy):
        return (
            jnp.clip(depth + dz, 0, ND - 1) if dz else depth,
            jnp.clip(group + dy, 0, NG - 1) if dy else group,
        )

    loads = [
        pltpu.make_async_copy(src, dst, in_sem.at[n])
        for n, (src, dst) in enumerate(((o1, n_o1), (c2, n_c2), (o2, n_o2), (c1, n_c1)))
    ]
    for load in loads:
        load.start()

    barrier = pltpu.get_barrier_semaphore()

    def greet_depth(k, _):
        pl.semaphore_signal(
            barrier, inc=1, device_id=(lax.rem(depth + k, ND), group), device_id_type=MESH
        )
        return 0

    def greet_group(k, _):
        pl.semaphore_signal(
            barrier, inc=1, device_id=(depth, lax.rem(group + k, NG)), device_id_type=MESH
        )
        return 0

    lax.fori_loop(1, ND, greet_depth, 0)
    lax.fori_loop(1, NG, greet_group, 0)
    for dz, dy in DIRS:
        if dz != 0 and dy != 0:

            @pl.when(exists(dz, dy))
            def _():
                pl.semaphore_signal(barrier, inc=1, device_id=clamp(dz, dy), device_id_type=MESH)

    perm[...] = permutation()
    place = lane() >> 4
    mask = jnp.zeros((1, NX), F32)
    for slot in range(8):
        mask = jnp.where(place == bricks_ref[0, group, slot], 1.0, mask)

    volumes = (p_u, p_l, p_eg, p_ef)

    def zero_plane(ref, z):
        def body(y, _):
            ref[z, y] = jnp.zeros((CH, NX), BF)
            return 0

        lax.fori_loop(0, B + 2, body, 0)

    def zero_row(ref, y):
        def body(z, _):
            ref[z, y] = jnp.zeros((CH, NX), BF)
            return 0

        lax.fori_loop(0, B + 2, body, 0)

    for d, at in ((depth == 0, 0), (depth == ND - 1, B + 1)):

        @pl.when(d)
        def _():
            for ref in volumes:
                zero_plane(ref, at)

    for d, at in ((group == 0, 0), (group == NG - 1, B + 1)):

        @pl.when(d)
        def _():
            for ref in volumes:
                zero_row(ref, at)

    def relayout(src, dst, masked=None):
        def body(k, _):
            for h in range(2):
                pair = jnp.concatenate(
                    [src[pl.ds(16 * h, 16), 2 * k + zz].reshape(256, NX) for zz in range(2)], axis=1
                )
                turned = dot(perm[...], pair)
                for zz in range(2):
                    half = turned[:, NX * zz : NX * (zz + 1)]
                    dst[2 * k + zz, :, 16 * h : 16 * h + 16, :] = half.astype(BF).reshape(16, 16, NX)
                    if masked is not None:
                        masked[2 * k + 1 + zz, 1 : B + 1, 16 * h : 16 * h + 16, :] = (
                            (half * mask).astype(BF).reshape(16, 16, NX)
                        )
            return 0

        lax.fori_loop(0, 8, body, 0)

    def side(d, sending):
        if d == 0:
            return pl.ds(1, B)
        if sending:
            return pl.ds(B if d > 0 else 1, 1)
        return pl.ds(0 if d > 0 else B + 1, 1)

    def halo(number, k):
        dz, dy = DIRS[k]
        ref = volumes[number]
        return pltpu.make_async_remote_copy(
            src_ref=ref.at[side(dz, True), side(dy, True)],
            dst_ref=ref.at[side(dz, False), side(dy, False)],
            send_sem=hs.at[number, k],
            recv_sem=hr.at[number, k],
            device_id=clamp(dz, dy),
            device_id_type=MESH,
        )

    def halo_start(number):
        for k, (dz, dy) in enumerate(DIRS):

            @pl.when(exists(dz, dy))
            def _():
                halo(number, k).start()

    def halo_arrived(number):
        for k, (dz, dy) in enumerate(DIRS):

            @pl.when(exists(-dz, -dy))
            def _():
                halo(number, k).wait_recv()

    def halo_sent(number):
        for k, (dz, dy) in enumerate(DIRS):

            @pl.when(exists(dz, dy))
            def _():
                halo(number, k).wait_send()

    def windows(ref, i, q):
        return jnp.concatenate(
            [ref[pl.ds(2 * i, 4), pl.ds(4 * q + 2 * r, 4)].reshape(512, NX) for r in range(2)],
            axis=1,
        )

    def join(product, r):
        cut = product[:, NX * r : NX * (r + 1)]
        return cut[128:256] + shift_up(cut[0:128]) + shift_down(cut[256:384])

    def get(ref, i, j):
        return ref[pl.ds(2 * i, 2), pl.ds(2 * j, 2)].reshape(128, NX).astype(F32)

    def put(ref, i, j, values):
        ref[pl.ds(2 * i, 2), pl.ds(2 * j, 2)] = values.reshape(2, 2, CH, NX)

    def put_inner(ref, i, j, values):
        ref[pl.ds(2 * i + 1, 2), pl.ds(2 * j + 1, 2)] = values.reshape(2, 2, CH, NX)

    def put_shifted(i, j, errors):
        wide = errors.astype(F32)
        for number, moved in enumerate((shift_down(wide), shift_up(wide))):
            shifted[number, pl.ds(2 * i, 2), pl.ds(2 * j, 2)] = moved.astype(BF).reshape(2, 2, CH, NX)

    def over_patches(body):
        def step(n, _):
            body(lax.div(n, 4), lax.rem(n, 4))
            return 0

        lax.fori_loop(0, 32, step, 0)

    def sigmoid(v):
        return 0.5 + 0.5 * jnp.tanh(0.5 * v)

    def weight_gradient(w, errors_ref, source_ref):
        acc[...] = jnp.zeros_like(acc)

        def body(i, _):
            left, right = [], []
            for j in range(8):
                low = shifted[0, pl.ds(2 * i, 2), 2 * j : 2 * j + 2].reshape(128, NX)
                mid = errors_ref[pl.ds(2 * i + 1, 2), 2 * j + 1 : 2 * j + 3].reshape(128, NX)
                top = shifted[1, pl.ds(2 * i, 2), 2 * j : 2 * j + 2].reshape(128, NX)
                left.append(jnp.concatenate([low, mid, top], axis=0))
                right.append(source_ref[pl.ds(2 * i, 4), 2 * j : 2 * j + 4].reshape(512, NX))
            acc[...] += dot_nt(jnp.concatenate(left, axis=1), jnp.concatenate(right, axis=1))
            return 0

        lax.fori_loop(0, 8, body, 0)
        for c in range(3):
            total = None
            for zo in range(2):
                for yo in range(2):
                    row = (c * 4 + zo * 2 + yo) * CH
                    turn = (zo * 4 + yo) * CH
                    rows = acc[row : row + CH, :]
                    if turn:
                        rows = pltpu.roll(rows, 512 - turn, 1)
                    total = rows if total is None else total + rows
            part[w, 4 * c : 4 * c + 4] = total[:, :384].reshape(4, 8, 384)

    def rs_copy(w, k):
        peer = lax.rem(depth + k, ND)
        return pltpu.make_async_remote_copy(
            src_ref=part.at[w, lax.rem(peer, CHUNKS)],
            dst_ref=rs_in.at[w, depth],
            send_sem=rs_s.at[w, k],
            recv_sem=rs_r.at[w, depth],
            device_id=(peer, group),
            device_id_type=MESH,
        )

    def rs_arrival(w, k):
        peer = lax.rem(depth + k, ND)
        return pltpu.make_async_remote_copy(
            src_ref=part.at[w, 0],
            dst_ref=rs_in.at[w, peer],
            send_sem=rs_s.at[w, k],
            recv_sem=rs_r.at[w, peer],
            device_id=(peer, group),
            device_id_type=MESH,
        )

    def ar_copy(w, k):
        peer = lax.rem(group + k, NG)
        return pltpu.make_async_remote_copy(
            src_ref=ar_in.at[w, group],
            dst_ref=ar_in.at[w, group],
            send_sem=ar_s.at[w, k],
            recv_sem=ar_r.at[w, group],
            device_id=(depth, peer),
            device_id_type=MESH,
        )

    def ar_arrival(w, k):
        peer = lax.rem(group + k, NG)
        return pltpu.make_async_remote_copy(
            src_ref=ar_in.at[w, group],
            dst_ref=ar_in.at[w, peer],
            send_sem=ar_s.at[w, k],
            recv_sem=ar_r.at[w, peer],
            device_id=(depth, peer),
            device_id_type=MESH,
        )

    def ag_copy(w, k):
        peer = lax.rem(depth + k, ND)
        return pltpu.make_async_remote_copy(
            src_ref=tot.at[w, lax.rem(depth, CHUNKS)],
            dst_ref=tot.at[w, lax.rem(depth, CHUNKS)],
            send_sem=ag_s.at[w, k],
            recv_sem=ag_r.at[w, lax.rem(depth, CHUNKS)],
            device_id=(peer, group),
            device_id_type=MESH,
        )

    def ag_arrival(w, k):
        peer = lax.rem(depth + k, ND)
        at = lax.rem(peer, CHUNKS)
        return pltpu.make_async_remote_copy(
            src_ref=tot.at[w, at],
            dst_ref=tot.at[w, at],
            send_sem=ag_s.at[w, k],
            recv_sem=ag_r.at[w, at],
            device_id=(peer, group),
            device_id_type=MESH,
        )

    owner = depth < CHUNKS

    def each_peer(size, act, only_owners=False):
        def body(k, _):
            if only_owners:

                @pl.when(lax.rem(depth + k, ND) < CHUNKS)
                def _():
                    act(k)
            else:
                act(k)
            return 0

        lax.fori_loop(1, size, body, 0)

    def reduce_start(w):
        each_peer(ND, lambda k: rs_copy(w, k).start(), True)

    def reduce_middle(w):
        @pl.when(owner)
        def _():
            rs_in[w, depth] = part[w, lax.rem(depth, CHUNKS)]
            each_peer(ND, lambda k: rs_arrival(w, k).wait_recv())
            ar_in[w, group] = jnp.sum(rs_in[w], axis=0)
            each_peer(NG, lambda k: ar_copy(w, k).start())

    def reduce_spread(w):
        @pl.when(owner)
        def _():
            each_peer(NG, lambda k: ar_arrival(w, k).wait_recv())
            tot[w, lax.rem(depth, CHUNKS)] = jnp.sum(ar_in[w], axis=0)
            each_peer(ND, lambda k: ag_copy(w, k).start())

    def reduce_end(w):
        each_peer(ND, lambda k: ag_arrival(w, k).wait_recv(), True)
        each_peer(ND, lambda k: rs_copy(w, k).wait_send(), True)

        @pl.when(owner)
        def _():
            each_peer(NG, lambda k: ar_copy(w, k).wait_send())
            each_peer(ND, lambda k: ag_copy(w, k).wait_send())

    build_band(w2_ref, band_g)
    loads[0].wait()
    relayout(n_o1, q_o1, p_u)
    near = jnp.minimum(depth, 1) + jnp.minimum(ND - 1 - depth, 1)
    aside = jnp.minimum(group, 1) + jnp.minimum(NG - 1 - group, 1)
    pl.semaphore_wait(barrier, ND - 1 + NG - 1 + near * aside)
    halo_start(0)
    loads[1].wait()
    relayout(n_c2, q_c2)
    loads[2].wait()
    relayout(n_o2, q_o2)
    loads[3].wait()
    relayout(n_c1, q_c1)
    build_band(w1_ref, band_f)
    build_band_transposed(w1_ref, band_tf)
    build_band_transposed(w2_ref, band_tg)
    halo_arrived(0)

    def first(i, q):
        product = dot(band_g[...], windows(p_u, i, q))
        for r in range(2):
            j = 2 * q + r
            v = join(product, r)
            s = sigmoid(v)
            silu = v * s
            shaped = (mask * silu).astype(BF).astype(F32)
            slope = s + silu * (1.0 - s)
            errors = (mask * get(q_c2, i, j) * slope).astype(BF)
            restored = (get(q_o2, i, j) - shaped).astype(BF)
            put(q_o2, i, j, restored)
            put_inner(p_l, i, j, (restored.astype(F32) * mask).astype(BF))
            put_inner(p_eg, i, j, errors)
            put_shifted(i, j, errors)

    over_patches(first)
    halo_start(1)
    halo_start(2)
    out_two = pltpu.make_async_copy(q_o2, r2_out, out_sem.at[0])
    out_two.start()
    weight_gradient(0, p_eg, p_u)
    reduce_start(0)
    halo_arrived(1)
    halo_arrived(2)

    def second(i, q):
        spread = dot(band_tg[...], windows(p_eg, i, q))
        product = dot(band_f[...], windows(p_l, i, q))
        for r in range(2):
            j = 2 * q + r
            total = (get(q_c1, i, j) + mask * join(spread, r)).astype(BF)
            put(q_c1, i, j, total)
            v = join(product, r)
            s = sigmoid(v)
            silu = v * s
            shaped = (mask * silu).astype(BF).astype(F32)
            slope = s + silu * (1.0 - s)
            errors = (mask * total.astype(F32) * slope).astype(BF)
            put(q_o1, i, j, (get(q_o1, i, j) - shaped).astype(BF))
            put_inner(p_ef, i, j, errors)
            put_shifted(i, j, errors)

    over_patches(second)
    halo_start(3)
    out_one = pltpu.make_async_copy(q_o1, r1_out, out_sem.at[1])
    out_one.start()
    out_grad = pltpu.make_async_copy(q_c1, g1_out, out_sem.at[2])
    out_grad.start()
    reduce_middle(0)
    weight_gradient(1, p_ef, p_l)
    reduce_start(1)
    reduce_spread(0)
    halo_arrived(3)

    def third(i, q):
        spread = dot(band_tf[...], windows(p_ef, i, q))
        for r in range(2):
            j = 2 * q + r
            put(q_c2, i, j, (get(q_c2, i, j) + mask * join(spread, r)).astype(BF))

    over_patches(third)
    out_last = pltpu.make_async_copy(q_c2, g2_out, out_sem.at[3])
    out_last.start()
    reduce_middle(1)
    reduce_spread(1)
    reduce_end(0)
    reduce_end(1)
    for number in range(4):
        halo_sent(number)
    t2_out[...] = tot[0]
    t1_out[...] = tot[1]
    for copy in (out_two, out_one, out_grad, out_last):
        copy.wait()


def natural(scale, r1, r2, g1, g2, t1, t2, r1_out, r2_out, g1_out, g2_out, w1_out, w2_out):
    perm = permutation()
    for src, dst in ((r1, r1_out), (r2, r2_out), (g1, g1_out), (g2, g2_out)):
        for h in range(2):
            pair = jnp.concatenate(
                [src[zz, :, 16 * h : 16 * h + 16, :].reshape(256, NX) for zz in range(2)], axis=1
            )
            turned = dot(perm, pair)
            for zz in range(2):
                half = turned[:, NX * zz : NX * (zz + 1)]
                dst[16 * h : 16 * h + 16, zz] = half.astype(BF).reshape(16, 16, NX)

    @pl.when(pl.program_id(0) == 0)
    def _():
        for src, dst in ((t1, w1_out), (t2, w2_out)):
            for c in range(3):
                rows = src[4 * c : 4 * c + 4].reshape(CH, 384) * scale
                for a in range(3):
                    for b in range(3):
                        at = (a * 4 + b) * CH
                        dst[9 * a + 3 * b + c] = rows[:, at : at + CH]


def local(output_one, output_two, cotangent_one, cotangent_two, first_weight, second_weight, bricks):
    turned = jax.ShapeDtypeStruct((B, B, CH, NX), BF)
    sums = jax.ShapeDtypeStruct((CHUNKS, 8, 384), F32)
    hbm = pl.BlockSpec(memory_space=pl.ANY)
    vmem = pl.BlockSpec(memory_space=pltpu.VMEM)
    smem = pl.BlockSpec(memory_space=pltpu.SMEM)
    plain = pltpu.VMEM((CH, B, B, NX), BF)
    flipped = pltpu.VMEM((B, B, CH, NX), BF)
    padded = pltpu.VMEM((B + 2, B + 2, CH, NX), BF)
    band = pltpu.VMEM((384, 512), BF)
    dma = pltpu.SemaphoreType.DMA
    r1, r2, g1, g2, t1, t2 = pl.pallas_call(
        fused,
        out_shape=(turned, turned, turned, turned, sums, sums),
        in_specs=[hbm, hbm, hbm, hbm, vmem, vmem, smem],
        out_specs=(hbm, hbm, hbm, hbm, vmem, vmem),
        scratch_shapes=[plain] * 4
        + [flipped] * 4
        + [padded] * 4
        + [
            pltpu.VMEM((2, B, B, CH, NX), BF),
            pltpu.VMEM((256, 256), BF),
            band,
            band,
            band,
            band,
            pltpu.VMEM((384, 512), F32),
            pltpu.VMEM((2, CHUNKS, 8, 384), F32),
            pltpu.VMEM((2, ND, 8, 384), F32),
            pltpu.VMEM((2, NG, 8, 384), F32),
            pltpu.VMEM((2, CHUNKS, 8, 384), F32),
            dma((4,)),
            dma((4,)),
            dma((4, 8)),
            dma((4, 8)),
            dma((2, ND)),
            dma((2, ND)),
            dma((2, NG)),
            dma((2, NG)),
            dma((2, ND)),
            dma((2, CHUNKS)),
        ],
        compiler_params=pltpu.CompilerParams(
            collective_id=0, has_side_effects=True, vmem_limit_bytes=56 * 1024 * 1024
        ),
        name="fused",
    )(output_one, output_two, cotangent_one, cotangent_two, first_weight, second_weight, bricks)

    scale = 1.0 / math.sqrt(float(B * ND * B * NG * NX))
    block = pl.BlockSpec((2, B, CH, NX), lambda k: (k, 0, 0, 0))
    result = pl.BlockSpec((CH, 2, B, NX), lambda k: (0, k, 0, 0))
    whole = pl.BlockSpec((CHUNKS, 8, 384), lambda k: (0, 0, 0))
    taps = pl.BlockSpec((27, CH, CH), lambda k: (0, 0, 0))
    volume = jax.ShapeDtypeStruct((CH, B, B, NX), BF)
    weight = jax.ShapeDtypeStruct((27, CH, CH), F32)

    def back(*refs):
        natural(scale, *refs)

    return pl.pallas_call(
        back,
        grid=(8,),
        out_shape=(volume, volume, volume, volume, weight, weight),
        in_specs=[block, block, block, block, whole, whole],
        out_specs=(result, result, result, result, taps, taps),
        name="natural",
    )(r1, r2, g1, g2, t1, t2)


def solution(mesh):
    slab = P(None, "depth", "group", None)
    return jax.shard_map(
        local,
        mesh=mesh,
        in_specs=(slab, slab, slab, slab, P(), P(), P("depth", None, None)),
        out_specs=(slab, slab, slab, slab, P(), P()),
        check_vma=False,
    )
```

```python
import math

import jax
import jax.numpy as jnp
from jax import lax
from jax.experimental import pallas as pl
from jax.experimental.pallas import tpu as pltpu
from jax.sharding import PartitionSpec as P

MESH = pl.DeviceIdType.MESH
BF = jnp.bfloat16
F32 = jnp.float32

CH = 32
B = 16
NX = 128
ND = 16
NG = 8
CHUNKS = 12
DIRS = tuple((dz, dy) for dz in (-1, 0, 1) for dy in (-1, 0, 1) if (dz, dy) != (0, 0))


def dot(a, b):
    return lax.dot_general(a, b, (((1,), (0,)), ((), ())), preferred_element_type=F32)


def dot_nt(a, b):
    return lax.dot_general(a, b, (((1,), (1,)), ((), ())), preferred_element_type=F32)


def permutation():
    row = lax.broadcasted_iota(jnp.int32, (256, 256), 0)
    col = lax.broadcasted_iota(jnp.int32, (256, 256), 1)
    return jnp.where((row & 15) * 16 + (row >> 4) == col, 1.0, 0.0).astype(BF)


def lane():
    return lax.broadcasted_iota(jnp.int32, (1, NX), 1)


def shift_up(values):
    return jnp.where(lane() == 0, 0.0, pltpu.roll(values, 1, 1))


def shift_down(values):
    return jnp.where(lane() == NX - 1, 0.0, pltpu.roll(values, NX - 1, 1))


def band_rows(blocks, out_ref):
    zeros = jnp.zeros((CH, NX), F32)
    for c in range(3):
        wide = jnp.concatenate([blocks(a, c) for a in range(3)] + [zeros], axis=1)
        for zo in range(2):
            for yo in range(2):
                turn = (zo * 4 + yo) * CH
                moved = wide if turn == 0 else pltpu.roll(wide, turn, 1)
                row = (c * 4 + zo * 2 + yo) * CH
                out_ref[row : row + CH, :] = moved.astype(BF)


def build_band(w_ref, out_ref):
    def blocks(a, c):
        taps = [w_ref[9 * a + 3 * b + c].astype(F32) for b in range(3)]
        return jnp.concatenate(taps + [jnp.zeros((CH, CH), F32)], axis=1)

    band_rows(blocks, out_ref)


def build_band_transposed(w_ref, out_ref):
    def blocks(a, c):
        taps = [w_ref[26 - (9 * a + 3 * b + c)].astype(F32) for b in range(3)]
        tall = jnp.concatenate(taps + [jnp.zeros((CH, CH), F32)], axis=0)
        square = jnp.concatenate([tall, jnp.zeros((NX, NX - CH), F32)], axis=1)
        return jnp.transpose(square)[:CH]

    band_rows(blocks, out_ref)


def fused(
    o1, o2, c1, c2, w1_ref, w2_ref, bricks_ref,
    r1_out, r2_out, g1_out, g2_out, t1_out, t2_out,
    n_o1, n_o2, n_c1, n_c2,
    q_o1, q_o2, q_c1, q_c2,
    p_u, p_l, p_eg, p_ef,
    shifted, perm, band_f, band_g, band_tf, band_tg, acc,
    part, rs_in, ar_in, tot,
    in_sem, out_sem, hs, hr, rs_s, rs_r, ar_s, ar_r, ag_s, ag_r,
):
    depth = lax.axis_index("depth")
    group = lax.axis_index("group")

    def exists(dz, dy):
        ok = None
        for d, at, size in ((dz, depth, ND), (dy, group, NG)):
            if d == 0:
                continue
            here = at > 0 if d < 0 else at < size - 1
            ok = here if ok is None else jnp.logical_and(ok, here)
        return ok

    def clamp(dz, dy):
        return (
            jnp.clip(depth + dz, 0, ND - 1) if dz else depth,
            jnp.clip(group + dy, 0, NG - 1) if dy else group,
        )

    loads = [
        pltpu.make_async_copy(src, dst, in_sem.at[n])
        for n, (src, dst) in enumerate(((o1, n_o1), (c2, n_c2), (o2, n_o2), (c1, n_c1)))
    ]
    for load in loads:
        load.start()

    barrier = pltpu.get_barrier_semaphore()

    def greet_depth(k, _):
        pl.semaphore_signal(
            barrier, inc=1, device_id=(lax.rem(depth + k, ND), group), device_id_type=MESH
        )
        return 0

    def greet_group(k, _):
        pl.semaphore_signal(
            barrier, inc=1, device_id=(depth, lax.rem(group + k, NG)), device_id_type=MESH
        )
        return 0

    lax.fori_loop(1, ND, greet_depth, 0)
    lax.fori_loop(1, NG, greet_group, 0)
    for dz, dy in DIRS:
        if dz != 0 and dy != 0:

            @pl.when(exists(dz, dy))
            def _():
                pl.semaphore_signal(barrier, inc=1, device_id=clamp(dz, dy), device_id_type=MESH)

    perm[...] = permutation()
    place = lane() >> 4
    mask = jnp.zeros((1, NX), F32)
    for slot in range(8):
        mask = jnp.where(place == bricks_ref[0, group, slot], 1.0, mask)

    volumes = (p_u, p_l, p_eg, p_ef)

    def zero_plane(ref, z):
        def body(y, _):
            ref[z, y] = jnp.zeros((CH, NX), BF)
            return 0

        lax.fori_loop(0, B + 2, body, 0)

    def zero_row(ref, y):
        def body(z, _):
            ref[z, y] = jnp.zeros((CH, NX), BF)
            return 0

        lax.fori_loop(0, B + 2, body, 0)

    for d, at in ((depth == 0, 0), (depth == ND - 1, B + 1)):

        @pl.when(d)
        def _():
            for ref in volumes:
                zero_plane(ref, at)

    for d, at in ((group == 0, 0), (group == NG - 1, B + 1)):

        @pl.when(d)
        def _():
            for ref in volumes:
                zero_row(ref, at)

    def relayout(src, dst, masked=None):
        def body(k, _):
            for h in range(2):
                pair = jnp.concatenate(
                    [src[pl.ds(16 * h, 16), 2 * k + zz].reshape(256, NX) for zz in range(2)], axis=1
                )
                turned = dot(perm[...], pair)
                for zz in range(2):
                    half = turned[:, NX * zz : NX * (zz + 1)]
                    dst[2 * k + zz, :, 16 * h : 16 * h + 16, :] = half.astype(BF).reshape(16, 16, NX)
                    if masked is not None:
                        masked[2 * k + 1 + zz, 1 : B + 1, 16 * h : 16 * h + 16, :] = (
                            (half * mask).astype(BF).reshape(16, 16, NX)
                        )
            return 0

        lax.fori_loop(0, 8, body, 0, unroll=8)

    def side(d, sending):
        if d == 0:
            return pl.ds(1, B)
        if sending:
            return pl.ds(B if d > 0 else 1, 1)
        return pl.ds(0 if d > 0 else B + 1, 1)

    def halo(number, k):
        dz, dy = DIRS[k]
        ref = volumes[number]
        return pltpu.make_async_remote_copy(
            src_ref=ref.at[side(dz, True), side(dy, True)],
            dst_ref=ref.at[side(dz, False), side(dy, False)],
            send_sem=hs.at[number, k],
            recv_sem=hr.at[number, k],
            device_id=clamp(dz, dy),
            device_id_type=MESH,
        )

    def halo_start(number):
        for k, (dz, dy) in enumerate(DIRS):

            @pl.when(exists(dz, dy))
            def _():
                halo(number, k).start()

    def halo_arrived(number):
        for k, (dz, dy) in enumerate(DIRS):

            @pl.when(exists(-dz, -dy))
            def _():
                halo(number, k).wait_recv()

    def halo_sent(number):
        for k, (dz, dy) in enumerate(DIRS):

            @pl.when(exists(dz, dy))
            def _():
                halo(number, k).wait_send()

    def windows(ref, i, pair):
        return jnp.concatenate(
            [ref[pl.ds(2 * i, 4), pl.ds(2 * j, 4)].reshape(512, NX) for j in pair], axis=1
        )

    def join(product, r):
        cut = product[:, NX * r : NX * (r + 1)]
        return cut[128:256] + shift_up(cut[0:128]) + shift_down(cut[256:384])

    def get(ref, i, j):
        return ref[pl.ds(2 * i, 2), pl.ds(2 * j, 2)].reshape(128, NX).astype(F32)

    def put(ref, i, j, values):
        ref[pl.ds(2 * i, 2), pl.ds(2 * j, 2)] = values.reshape(2, 2, CH, NX)

    def put_inner(ref, i, j, values):
        ref[pl.ds(2 * i + 1, 2), pl.ds(2 * j + 1, 2)] = values.reshape(2, 2, CH, NX)

    def put_shifted(i, j, errors):
        wide = errors.astype(F32)
        for number, moved in enumerate((shift_down(wide), shift_up(wide))):
            shifted[number, pl.ds(2 * i, 2), pl.ds(2 * j, 2)] = moved.astype(BF).reshape(2, 2, CH, NX)

    def inner_patches(body):
        def step(i, _):
            for j in (1, 3, 5):
                body(i, (j, j + 1))
            return 0

        lax.fori_loop(1, 7, step, 0, unroll=6)

    def outer_patches(body):
        def sides(i, _):
            body(i, (0, 7))
            return 0

        def ends(n, _):
            j = 2 * lax.rem(n, 4)
            body(7 * lax.div(n, 4), (j, j + 1))
            return 0

        lax.fori_loop(1, 7, sides, 0, unroll=6)
        lax.fori_loop(0, 8, ends, 0, unroll=8)

    def sigmoid(v):
        return 0.5 + 0.5 * jnp.tanh(0.5 * v)

    def weight_gradient(w, errors_ref, source_ref):
        acc[...] = jnp.zeros_like(acc)

        def body(i, _):
            left, right = [], []
            for j in range(8):
                low = shifted[0, pl.ds(2 * i, 2), 2 * j : 2 * j + 2].reshape(128, NX)
                mid = errors_ref[pl.ds(2 * i + 1, 2), 2 * j + 1 : 2 * j + 3].reshape(128, NX)
                top = shifted[1, pl.ds(2 * i, 2), 2 * j : 2 * j + 2].reshape(128, NX)
                left.append(jnp.concatenate([low, mid, top], axis=0))
                right.append(source_ref[pl.ds(2 * i, 4), 2 * j : 2 * j + 4].reshape(512, NX))
            acc[...] += dot_nt(jnp.concatenate(left, axis=1), jnp.concatenate(right, axis=1))
            return 0

        lax.fori_loop(0, 8, body, 0, unroll=4)
        for c in range(3):
            total = None
            for zo in range(2):
                for yo in range(2):
                    row = (c * 4 + zo * 2 + yo) * CH
                    turn = (zo * 4 + yo) * CH
                    rows = acc[row : row + CH, :]
                    if turn:
                        rows = pltpu.roll(rows, 512 - turn, 1)
                    total = rows if total is None else total + rows
            part[w, 4 * c : 4 * c + 4] = total[:, :384].reshape(4, 8, 384)

    def rs_copy(w, k):
        peer = lax.rem(depth + k, ND)
        return pltpu.make_async_remote_copy(
            src_ref=part.at[w, lax.rem(peer, CHUNKS)],
            dst_ref=rs_in.at[w, depth],
            send_sem=rs_s.at[w, k],
            recv_sem=rs_r.at[w, depth],
            device_id=(peer, group),
            device_id_type=MESH,
        )

    def rs_arrival(w, k):
        peer = lax.rem(depth + k, ND)
        return pltpu.make_async_remote_copy(
            src_ref=part.at[w, 0],
            dst_ref=rs_in.at[w, peer],
            send_sem=rs_s.at[w, k],
            recv_sem=rs_r.at[w, peer],
            device_id=(peer, group),
            device_id_type=MESH,
        )

    def ar_copy(w, k):
        peer = lax.rem(group + k, NG)
        return pltpu.make_async_remote_copy(
            src_ref=ar_in.at[w, group],
            dst_ref=ar_in.at[w, group],
            send_sem=ar_s.at[w, k],
            recv_sem=ar_r.at[w, group],
            device_id=(depth, peer),
            device_id_type=MESH,
        )

    def ar_arrival(w, k):
        peer = lax.rem(group + k, NG)
        return pltpu.make_async_remote_copy(
            src_ref=ar_in.at[w, group],
            dst_ref=ar_in.at[w, peer],
            send_sem=ar_s.at[w, k],
            recv_sem=ar_r.at[w, peer],
            device_id=(depth, peer),
            device_id_type=MESH,
        )

    def ag_copy(w, k):
        peer = lax.rem(depth + k, ND)
        return pltpu.make_async_remote_copy(
            src_ref=tot.at[w, lax.rem(depth, CHUNKS)],
            dst_ref=tot.at[w, lax.rem(depth, CHUNKS)],
            send_sem=ag_s.at[w, k],
            recv_sem=ag_r.at[w, lax.rem(depth, CHUNKS)],
            device_id=(peer, group),
            device_id_type=MESH,
        )

    def ag_arrival(w, k):
        peer = lax.rem(depth + k, ND)
        at = lax.rem(peer, CHUNKS)
        return pltpu.make_async_remote_copy(
            src_ref=tot.at[w, at],
            dst_ref=tot.at[w, at],
            send_sem=ag_s.at[w, k],
            recv_sem=ag_r.at[w, at],
            device_id=(peer, group),
            device_id_type=MESH,
        )

    owner = depth < CHUNKS

    def each_peer(size, act, only_owners=False):
        def body(k, _):
            if only_owners:

                @pl.when(lax.rem(depth + k, ND) < CHUNKS)
                def _():
                    act(k)
            else:
                act(k)
            return 0

        lax.fori_loop(1, size, body, 0)

    def reduce_start(w):
        each_peer(ND, lambda k: rs_copy(w, k).start(), True)

    def reduce_middle(w):
        @pl.when(owner)
        def _():
            rs_in[w, depth] = part[w, lax.rem(depth, CHUNKS)]
            each_peer(ND, lambda k: rs_arrival(w, k).wait_recv())
            ar_in[w, group] = jnp.sum(rs_in[w], axis=0)
            each_peer(NG, lambda k: ar_copy(w, k).start())

    def reduce_spread(w):
        @pl.when(owner)
        def _():
            each_peer(NG, lambda k: ar_arrival(w, k).wait_recv())
            tot[w, lax.rem(depth, CHUNKS)] = jnp.sum(ar_in[w], axis=0)
            each_peer(ND, lambda k: ag_copy(w, k).start())

    def reduce_end(w):
        each_peer(ND, lambda k: ag_arrival(w, k).wait_recv(), True)
        each_peer(ND, lambda k: rs_copy(w, k).wait_send(), True)

        @pl.when(owner)
        def _():
            each_peer(NG, lambda k: ar_copy(w, k).wait_send())
            each_peer(ND, lambda k: ag_copy(w, k).wait_send())

    build_band(w2_ref, band_g)
    loads[0].wait()
    relayout(n_o1, q_o1, p_u)
    near = jnp.minimum(depth, 1) + jnp.minimum(ND - 1 - depth, 1)
    aside = jnp.minimum(group, 1) + jnp.minimum(NG - 1 - group, 1)
    pl.semaphore_wait(barrier, ND - 1 + NG - 1 + near * aside)
    halo_start(0)
    loads[1].wait()
    relayout(n_c2, q_c2)
    loads[2].wait()
    relayout(n_o2, q_o2)
    loads[3].wait()
    relayout(n_c1, q_c1)
    build_band(w1_ref, band_f)
    build_band_transposed(w1_ref, band_tf)
    build_band_transposed(w2_ref, band_tg)

    def first(i, pair):
        product = dot(band_g[...], windows(p_u, i, pair))
        for r, j in enumerate(pair):
            v = join(product, r)
            s = sigmoid(v)
            silu = v * s
            shaped = (mask * silu).astype(BF).astype(F32)
            slope = s + silu * (1.0 - s)
            errors = (mask * get(q_c2, i, j) * slope).astype(BF)
            restored = (get(q_o2, i, j) - shaped).astype(BF)
            put(q_o2, i, j, restored)
            put_inner(p_l, i, j, (restored.astype(F32) * mask).astype(BF))
            put_inner(p_eg, i, j, errors)
            put_shifted(i, j, errors)

    inner_patches(first)
    halo_arrived(0)
    outer_patches(first)
    halo_start(1)
    halo_start(2)
    out_two = pltpu.make_async_copy(q_o2, r2_out, out_sem.at[0])
    out_two.start()
    weight_gradient(0, p_eg, p_u)
    reduce_start(0)

    def second(i, pair):
        spread = dot(band_tg[...], windows(p_eg, i, pair))
        product = dot(band_f[...], windows(p_l, i, pair))
        for r, j in enumerate(pair):
            total = (get(q_c1, i, j) + mask * join(spread, r)).astype(BF)
            put(q_c1, i, j, total)
            v = join(product, r)
            s = sigmoid(v)
            silu = v * s
            shaped = (mask * silu).astype(BF).astype(F32)
            slope = s + silu * (1.0 - s)
            errors = (mask * total.astype(F32) * slope).astype(BF)
            put(q_o1, i, j, (get(q_o1, i, j) - shaped).astype(BF))
            put_inner(p_ef, i, j, errors)
            put_shifted(i, j, errors)

    inner_patches(second)
    halo_arrived(1)
    halo_arrived(2)
    outer_patches(second)
    halo_start(3)
    out_one = pltpu.make_async_copy(q_o1, r1_out, out_sem.at[1])
    out_one.start()
    out_grad = pltpu.make_async_copy(q_c1, g1_out, out_sem.at[2])
    out_grad.start()
    reduce_middle(0)
    weight_gradient(1, p_ef, p_l)
    reduce_start(1)
    reduce_spread(0)

    def third(i, pair):
        spread = dot(band_tf[...], windows(p_ef, i, pair))
        for r, j in enumerate(pair):
            put(q_c2, i, j, (get(q_c2, i, j) + mask * join(spread, r)).astype(BF))

    inner_patches(third)
    halo_arrived(3)
    outer_patches(third)
    out_last = pltpu.make_async_copy(q_c2, g2_out, out_sem.at[3])
    out_last.start()
    reduce_middle(1)
    reduce_spread(1)
    reduce_end(0)
    reduce_end(1)
    for number in range(4):
        halo_sent(number)
    t2_out[...] = tot[0]
    t1_out[...] = tot[1]
    for copy in (out_two, out_one, out_grad, out_last):
        copy.wait()


def natural(scale, r1, r2, g1, g2, t1, t2, r1_out, r2_out, g1_out, g2_out, w1_out, w2_out):
    perm = permutation()
    for src, dst in ((r1, r1_out), (r2, r2_out), (g1, g1_out), (g2, g2_out)):
        for h in range(2):
            pair = jnp.concatenate(
                [src[zz, :, 16 * h : 16 * h + 16, :].reshape(256, NX) for zz in range(2)], axis=1
            )
            turned = dot(perm, pair)
            for zz in range(2):
                half = turned[:, NX * zz : NX * (zz + 1)]
                dst[16 * h : 16 * h + 16, zz] = half.astype(BF).reshape(16, 16, NX)

    @pl.when(pl.program_id(0) == 0)
    def _():
        for src, dst in ((t1, w1_out), (t2, w2_out)):
            for c in range(3):
                rows = src[4 * c : 4 * c + 4].reshape(CH, 384) * scale
                for a in range(3):
                    for b in range(3):
                        at = (a * 4 + b) * CH
                        dst[9 * a + 3 * b + c] = rows[:, at : at + CH]


def local(output_one, output_two, cotangent_one, cotangent_two, first_weight, second_weight, bricks):
    turned = jax.ShapeDtypeStruct((B, B, CH, NX), BF)
    sums = jax.ShapeDtypeStruct((CHUNKS, 8, 384), F32)
    hbm = pl.BlockSpec(memory_space=pl.ANY)
    vmem = pl.BlockSpec(memory_space=pltpu.VMEM)
    smem = pl.BlockSpec(memory_space=pltpu.SMEM)
    plain = pltpu.VMEM((CH, B, B, NX), BF)
    flipped = pltpu.VMEM((B, B, CH, NX), BF)
    padded = pltpu.VMEM((B + 2, B + 2, CH, NX), BF)
    band = pltpu.VMEM((384, 512), BF)
    dma = pltpu.SemaphoreType.DMA
    r1, r2, g1, g2, t1, t2 = pl.pallas_call(
        fused,
        out_shape=(turned, turned, turned, turned, sums, sums),
        in_specs=[hbm, hbm, hbm, hbm, vmem, vmem, smem],
        out_specs=(hbm, hbm, hbm, hbm, vmem, vmem),
        scratch_shapes=[plain] * 4
        + [flipped] * 4
        + [padded] * 4
        + [
            pltpu.VMEM((2, B, B, CH, NX), BF),
            pltpu.VMEM((256, 256), BF),
            band,
            band,
            band,
            band,
            pltpu.VMEM((384, 512), F32),
            pltpu.VMEM((2, CHUNKS, 8, 384), F32),
            pltpu.VMEM((2, ND, 8, 384), F32),
            pltpu.VMEM((2, NG, 8, 384), F32),
            pltpu.VMEM((2, CHUNKS, 8, 384), F32),
            dma((4,)),
            dma((4,)),
            dma((4, 8)),
            dma((4, 8)),
            dma((2, ND)),
            dma((2, ND)),
            dma((2, NG)),
            dma((2, NG)),
            dma((2, ND)),
            dma((2, CHUNKS)),
        ],
        compiler_params=pltpu.CompilerParams(
            collective_id=0, has_side_effects=True, vmem_limit_bytes=56 * 1024 * 1024
        ),
        name="fused",
    )(output_one, output_two, cotangent_one, cotangent_two, first_weight, second_weight, bricks)

    scale = 1.0 / math.sqrt(float(B * ND * B * NG * NX))
    block = pl.BlockSpec((2, B, CH, NX), lambda k: (k, 0, 0, 0))
    result = pl.BlockSpec((CH, 2, B, NX), lambda k: (0, k, 0, 0))
    whole = pl.BlockSpec((CHUNKS, 8, 384), lambda k: (0, 0, 0))
    taps = pl.BlockSpec((27, CH, CH), lambda k: (0, 0, 0))
    volume = jax.ShapeDtypeStruct((CH, B, B, NX), BF)
    weight = jax.ShapeDtypeStruct((27, CH, CH), F32)

    def back(*refs):
        natural(scale, *refs)

    return pl.pallas_call(
        back,
        grid=(8,),
        out_shape=(volume, volume, volume, volume, weight, weight),
        in_specs=[block, block, block, block, whole, whole],
        out_specs=(result, result, result, result, taps, taps),
        name="natural",
    )(r1, r2, g1, g2, t1, t2)


def solution(mesh):
    slab = P(None, "depth", "group", None)
    return jax.shard_map(
        local,
        mesh=mesh,
        in_specs=(slab, slab, slab, slab, P(), P(), P("depth", None, None)),
        out_specs=(slab, slab, slab, slab, P(), P()),
        check_vma=False,
    )
```

```python
import math

import jax
import jax.numpy as jnp
from jax import lax
from jax.experimental import pallas as pl
from jax.experimental.pallas import tpu as pltpu
from jax.sharding import PartitionSpec as P

MESH = pl.DeviceIdType.MESH
BF = jnp.bfloat16
F32 = jnp.float32

CH = 32
B = 16
NX = 128
ND = 16
NG = 8
CHUNKS = 12
DIRS = ((0, -1), (0, 1), (-1, 0), (1, 0), (-1, -1), (-1, 1), (1, -1), (1, 1))
SIDES, ENDS, CORNERS = (0, 1), (2, 3), (4, 5, 6, 7)


def dot(a, b):
    return lax.dot_general(a, b, (((1,), (0,)), ((), ())), preferred_element_type=F32)


def dot_nt(a, b):
    return lax.dot_general(a, b, (((1,), (1,)), ((), ())), preferred_element_type=F32)


def permutation():
    row = lax.broadcasted_iota(jnp.int32, (256, 256), 0)
    col = lax.broadcasted_iota(jnp.int32, (256, 256), 1)
    return jnp.where((row & 15) * 16 + (row >> 4) == col, 1.0, 0.0).astype(BF)


def lane():
    return lax.broadcasted_iota(jnp.int32, (1, NX), 1)


def shift_up(values):
    return jnp.where(lane() == 0, 0.0, pltpu.roll(values, 1, 1))


def shift_down(values):
    return jnp.where(lane() == NX - 1, 0.0, pltpu.roll(values, NX - 1, 1))


def band_rows(blocks, out_ref):
    zeros = jnp.zeros((CH, NX), F32)
    for c in range(3):
        wide = jnp.concatenate([blocks(a, c) for a in range(3)] + [zeros], axis=1)
        for zo in range(2):
            for yo in range(2):
                turn = (zo * 4 + yo) * CH
                moved = wide if turn == 0 else pltpu.roll(wide, turn, 1)
                row = (c * 4 + zo * 2 + yo) * CH
                out_ref[row : row + CH, :] = moved.astype(BF)


def build_band(w_ref, out_ref):
    def blocks(a, c):
        taps = [w_ref[9 * a + 3 * b + c].astype(F32) for b in range(3)]
        return jnp.concatenate(taps + [jnp.zeros((CH, CH), F32)], axis=1)

    band_rows(blocks, out_ref)


def build_band_transposed(w_ref, out_ref):
    def blocks(a, c):
        taps = [w_ref[26 - (9 * a + 3 * b + c)].astype(F32) for b in range(3)]
        tall = jnp.concatenate(taps + [jnp.zeros((CH, CH), F32)], axis=0)
        square = jnp.concatenate([tall, jnp.zeros((NX, NX - CH), F32)], axis=1)
        return jnp.transpose(square)[:CH]

    band_rows(blocks, out_ref)


def fused(
    o1, o2, c1, c2, w1_ref, w2_ref, bricks_ref,
    q_o1, q_o2, q_c1, q_c2, t1_out, t2_out,
    n_o1, n_o2, n_c1, n_c2,
    p_u, p_pair, p_ef,
    shifted, perm, band_f, band_g, band_tf, band_tg, acc,
    part, rs_in, ar_in, tot,
    in_sem, hs, hr, rs_s, rs_r, ar_s, ar_r, ag_s, ag_r,
):
    depth = lax.axis_index("depth")
    group = lax.axis_index("group")

    def exists(dz, dy):
        ok = None
        for d, at, size in ((dz, depth, ND), (dy, group, NG)):
            if d == 0:
                continue
            here = at > 0 if d < 0 else at < size - 1
            ok = here if ok is None else jnp.logical_and(ok, here)
        return ok

    def clamp(dz, dy):
        return (
            jnp.clip(depth + dz, 0, ND - 1) if dz else depth,
            jnp.clip(group + dy, 0, NG - 1) if dy else group,
        )

    loads = [
        pltpu.make_async_copy(src, dst, in_sem.at[n])
        for n, (src, dst) in enumerate(((o1, n_o1), (c2, n_c2), (o2, n_o2), (c1, n_c1)))
    ]
    loads[0].start()

    barrier = pltpu.get_barrier_semaphore()

    def greet_depth(k, _):
        pl.semaphore_signal(
            barrier, inc=1, device_id=(lax.rem(depth + k, ND), group), device_id_type=MESH
        )
        return 0

    def greet_group(k, _):
        pl.semaphore_signal(
            barrier, inc=1, device_id=(depth, lax.rem(group + k, NG)), device_id_type=MESH
        )
        return 0

    lax.fori_loop(1, ND, greet_depth, 0, unroll=ND - 1)
    lax.fori_loop(1, NG, greet_group, 0, unroll=NG - 1)
    for dz, dy in DIRS:
        if dz != 0 and dy != 0:

            @pl.when(exists(dz, dy))
            def _():
                pl.semaphore_signal(barrier, inc=1, device_id=clamp(dz, dy), device_id_type=MESH)

    perm[...] = permutation()
    place = lane() >> 4
    mask = jnp.zeros((1, NX), F32)
    for slot in range(8):
        mask = jnp.where(place == bricks_ref[0, group, slot], 1.0, mask)

    p_l, p_eg = p_pair.at[0], p_pair.at[1]
    volumes = (p_u, p_pair, p_ef)

    def zero_plane(ref, z):
        def body(y, _):
            ref[z, y] = jnp.zeros((CH, NX), BF)
            return 0

        lax.fori_loop(0, B + 2, body, 0)

    def zero_row(ref, y):
        def body(z, _):
            ref[z, y] = jnp.zeros((CH, NX), BF)
            return 0

        lax.fori_loop(0, B + 2, body, 0)

    for d, at in ((depth == 0, 0), (depth == ND - 1, B + 1)):

        @pl.when(d)
        def _():
            for ref in (p_u, p_l, p_eg, p_ef):
                zero_plane(ref, at)

    for d, at in ((group == 0, 0), (group == NG - 1, B + 1)):

        @pl.when(d)
        def _():
            for ref in (p_u, p_l, p_eg, p_ef):
                zero_row(ref, at)

    def relayout(src, dst, masked=None):
        def body(k, _):
            for h in range(2):
                pair = jnp.concatenate(
                    [src[pl.ds(16 * h, 16), 2 * k + zz].reshape(256, NX) for zz in range(2)], axis=1
                )
                turned = dot(perm[...], pair)
                for zz in range(2):
                    half = turned[:, NX * zz : NX * (zz + 1)]
                    dst[2 * k + zz, :, 16 * h : 16 * h + 16, :] = half.astype(BF).reshape(16, 16, NX)
                    if masked is not None:
                        masked[2 * k + 1 + zz, 1 : B + 1, 16 * h : 16 * h + 16, :] = (
                            (half * mask).astype(BF).reshape(16, 16, NX)
                        )
            return 0

        lax.fori_loop(0, 8, body, 0, unroll=8)

    def side(d, sending):
        if d == 0:
            return pl.ds(1, B)
        if sending:
            return pl.ds(B if d > 0 else 1, 1)
        return pl.ds(0 if d > 0 else B + 1, 1)

    def halo(number, k):
        dz, dy = DIRS[k]
        ref = volumes[number]
        both = (pl.ds(0, 2),) if number == 1 else ()
        return pltpu.make_async_remote_copy(
            src_ref=ref.at[*both, side(dz, True), side(dy, True)],
            dst_ref=ref.at[*both, side(dz, False), side(dy, False)],
            send_sem=hs.at[number, k],
            recv_sem=hr.at[number, k],
            device_id=clamp(dz, dy),
            device_id_type=MESH,
        )

    def halo_start(number):
        for k, (dz, dy) in enumerate(DIRS):

            @pl.when(exists(dz, dy))
            def _():
                halo(number, k).start()

    def halo_arrived(number, which):
        for k in which:
            dz, dy = DIRS[k]

            @pl.when(exists(-dz, -dy))
            def _():
                halo(number, k).wait_recv()

    def halo_sent(number):
        for k, (dz, dy) in enumerate(DIRS):

            @pl.when(exists(dz, dy))
            def _():
                halo(number, k).wait_send()

    def windows(ref, i, pair):
        return jnp.concatenate(
            [ref[pl.ds(2 * i, 4), pl.ds(2 * j, 4)].reshape(512, NX) for j in pair], axis=1
        )

    def join(product, r):
        cut = product[:, NX * r : NX * (r + 1)]
        return cut[128:256] + shift_up(cut[0:128]) + shift_down(cut[256:384])

    def get(ref, i, j):
        return ref[pl.ds(2 * i, 2), pl.ds(2 * j, 2)].reshape(128, NX).astype(F32)

    def put(ref, i, j, values):
        ref[pl.ds(2 * i, 2), pl.ds(2 * j, 2)] = values.reshape(2, 2, CH, NX)

    def put_inner(ref, i, j, values):
        ref[pl.ds(2 * i + 1, 2), pl.ds(2 * j + 1, 2)] = values.reshape(2, 2, CH, NX)

    def put_shifted(i, j, errors):
        wide = errors.astype(F32)
        for number, moved in enumerate((shift_down(wide), shift_up(wide))):
            shifted[number, pl.ds(2 * i, 2), pl.ds(2 * j, 2)] = moved.astype(BF).reshape(2, 2, CH, NX)

    def inner_patches(body):
        def step(i, _):
            for j in (1, 3, 5):
                body(i, (j, j + 1))
            return 0

        lax.fori_loop(1, 7, step, 0, unroll=6)

    def outer_patches(body, number):
        def end(n, _):
            j = 2 * lax.rem(n, 3) + 1
            body(7 * lax.div(n, 3), (j, j + 1))
            return 0

        def edge(i, _):
            body(i, (0, 7))
            return 0

        halo_arrived(number, ENDS)
        lax.fori_loop(0, 6, end, 0, unroll=6)
        halo_arrived(number, SIDES)
        lax.fori_loop(1, 7, edge, 0, unroll=6)
        halo_arrived(number, CORNERS)
        body(0, (0, 7))
        body(7, (0, 7))

    def sigmoid(v):
        return 0.5 + 0.5 * jnp.tanh(0.5 * v)

    def weight_gradient(w, errors_ref, source_ref):
        acc[...] = jnp.zeros_like(acc)

        def body(i, _):
            left, right = [], []
            for j in range(8):
                low = shifted[0, pl.ds(2 * i, 2), 2 * j : 2 * j + 2].reshape(128, NX)
                mid = errors_ref[pl.ds(2 * i + 1, 2), 2 * j + 1 : 2 * j + 3].reshape(128, NX)
                top = shifted[1, pl.ds(2 * i, 2), 2 * j : 2 * j + 2].reshape(128, NX)
                left.append(jnp.concatenate([low, mid, top], axis=0))
                right.append(source_ref[pl.ds(2 * i, 4), 2 * j : 2 * j + 4].reshape(512, NX))
            acc[...] += dot_nt(jnp.concatenate(left, axis=1), jnp.concatenate(right, axis=1))
            return 0

        lax.fori_loop(0, 8, body, 0, unroll=4)
        for c in range(3):
            total = None
            for zo in range(2):
                for yo in range(2):
                    row = (c * 4 + zo * 2 + yo) * CH
                    turn = (zo * 4 + yo) * CH
                    rows = acc[row : row + CH, :]
                    if turn:
                        rows = pltpu.roll(rows, 512 - turn, 1)
                    total = rows if total is None else total + rows
            part[w, 4 * c : 4 * c + 4] = total[:, :384].reshape(4, 8, 384)

    own = lax.rem(depth, CHUNKS)
    owner = depth < CHUNKS

    def rs_copy(w, k):
        peer = lax.rem(depth + k, ND)
        return pltpu.make_async_remote_copy(
            src_ref=part.at[w, lax.rem(peer, CHUNKS)],
            dst_ref=rs_in.at[w, depth],
            send_sem=rs_s.at[w],
            recv_sem=rs_r.at[w],
            device_id=(peer, group),
            device_id_type=MESH,
        )

    def ar_copy(w, k):
        return pltpu.make_async_remote_copy(
            src_ref=ar_in.at[w, group],
            dst_ref=ar_in.at[w, group],
            send_sem=ar_s.at[w],
            recv_sem=ar_r.at[w],
            device_id=(depth, lax.rem(group + k, NG)),
            device_id_type=MESH,
        )

    def ag_copy(w, k):
        return pltpu.make_async_remote_copy(
            src_ref=tot.at[w, own],
            dst_ref=tot.at[w, own],
            send_sem=ag_s.at[w],
            recv_sem=ag_r.at[w],
            device_id=(lax.rem(depth + k, ND), group),
            device_id_type=MESH,
        )

    def await_chunks(sem, w, count):
        ref = rs_in.at[w, pl.ds(0, count)]
        pltpu.make_async_copy(ref, ref, sem.at[w]).wait()

    def each_peer(size, act, only_owners=False):
        def body(k, _):
            if only_owners:

                @pl.when(lax.rem(depth + k, ND) < CHUNKS)
                def _():
                    act(k)
            else:
                act(k)
            return 0

        lax.fori_loop(1, size, body, 0, unroll=size - 1)

    def reduce_start(w):
        each_peer(ND, lambda k: rs_copy(w, k).start(), True)

    def reduce_middle(w):
        @pl.when(owner)
        def _():
            rs_in[w, depth] = part[w, own]
            await_chunks(rs_r, w, ND - 1)
            ar_in[w, group] = jnp.sum(rs_in[w], axis=0)
            each_peer(NG, lambda k: ar_copy(w, k).start())

    def reduce_spread(w):
        @pl.when(owner)
        def _():
            await_chunks(ar_r, w, NG - 1)
            tot[w, own] = jnp.sum(ar_in[w], axis=0)
            each_peer(ND, lambda k: ag_copy(w, k).start())

    def reduce_end(w):
        @pl.when(owner)
        def _():
            await_chunks(ag_r, w, CHUNKS - 1)
            await_chunks(rs_s, w, CHUNKS - 1)
            await_chunks(ar_s, w, NG - 1)
            await_chunks(ag_s, w, ND - 1)

        @pl.when(jnp.logical_not(owner))
        def _():
            await_chunks(ag_r, w, CHUNKS)
            await_chunks(rs_s, w, CHUNKS)

    build_band(w2_ref, band_g)
    loads[0].wait()
    for load in loads[1:]:
        load.start()
    relayout(n_o1, q_o1, p_u)
    near = jnp.minimum(depth, 1) + jnp.minimum(ND - 1 - depth, 1)
    aside = jnp.minimum(group, 1) + jnp.minimum(NG - 1 - group, 1)
    pl.semaphore_wait(barrier, ND - 1 + NG - 1 + near * aside)
    halo_start(0)
    loads[1].wait()
    relayout(n_c2, q_c2)
    loads[2].wait()
    relayout(n_o2, q_o2)
    loads[3].wait()
    relayout(n_c1, q_c1)
    build_band(w1_ref, band_f)
    build_band_transposed(w1_ref, band_tf)
    build_band_transposed(w2_ref, band_tg)

    def first(i, pair):
        product = dot(band_g[...], windows(p_u, i, pair))
        for r, j in enumerate(pair):
            v = join(product, r)
            s = sigmoid(v)
            silu = v * s
            shaped = (mask * silu).astype(BF).astype(F32)
            slope = s + silu * (1.0 - s)
            errors = (mask * get(q_c2, i, j) * slope).astype(BF)
            restored = (get(q_o2, i, j) - shaped).astype(BF)
            put(q_o2, i, j, restored)
            put_inner(p_l, i, j, (restored.astype(F32) * mask).astype(BF))
            put_inner(p_eg, i, j, errors)
            put_shifted(i, j, errors)

    inner_patches(first)
    outer_patches(first, 0)
    halo_start(1)
    weight_gradient(0, p_eg, p_u)
    reduce_start(0)

    def second(i, pair):
        spread = dot(band_tg[...], windows(p_eg, i, pair))
        product = dot(band_f[...], windows(p_l, i, pair))
        for r, j in enumerate(pair):
            total = (get(q_c1, i, j) + mask * join(spread, r)).astype(BF)
            put(q_c1, i, j, total)
            v = join(product, r)
            s = sigmoid(v)
            silu = v * s
            shaped = (mask * silu).astype(BF).astype(F32)
            slope = s + silu * (1.0 - s)
            errors = (mask * total.astype(F32) * slope).astype(BF)
            put(q_o1, i, j, (get(q_o1, i, j) - shaped).astype(BF))
            put_inner(p_ef, i, j, errors)
            put_shifted(i, j, errors)

    inner_patches(second)
    reduce_middle(0)
    outer_patches(second, 1)
    halo_start(2)
    weight_gradient(1, p_ef, p_l)
    reduce_start(1)
    reduce_spread(0)

    def third(i, pair):
        spread = dot(band_tf[...], windows(p_ef, i, pair))
        for r, j in enumerate(pair):
            put(q_c2, i, j, (get(q_c2, i, j) + mask * join(spread, r)).astype(BF))

    inner_patches(third)
    reduce_middle(1)
    outer_patches(third, 2)
    reduce_spread(1)
    reduce_end(0)
    reduce_end(1)
    for number in range(3):
        halo_sent(number)
    t2_out[...] = tot[0]
    t1_out[...] = tot[1]


def natural(
    scale, r1, r2, g1, g2, t1, t2,
    r1_out, r2_out, g1_out, g2_out, w1_out, w2_out,
    n1, n2, n3, n4, perm, sems,
):
    perm[...] = permutation()
    copies = []
    for number, (src, wide, out) in enumerate(
        ((r1, n1, r1_out), (r2, n2, r2_out), (g1, n3, g1_out), (g2, n4, g2_out))
    ):
        for h in range(2):

            def body(k, _):
                pair = jnp.concatenate(
                    [src[2 * k + zz, :, 16 * h : 16 * h + 16, :].reshape(256, NX) for zz in range(2)],
                    axis=1,
                )
                turned = dot(perm[...], pair)
                for zz in range(2):
                    half = turned[:, NX * zz : NX * (zz + 1)]
                    wide[16 * h : 16 * h + 16, 2 * k + zz] = half.astype(BF).reshape(16, 16, NX)
                return 0

            lax.fori_loop(0, 8, body, 0, unroll=8)
            copy = pltpu.make_async_copy(
                wide.at[pl.ds(16 * h, 16)], out.at[pl.ds(16 * h, 16)], sems.at[number, h]
            )
            copy.start()
            copies.append(copy)
    for src, dst in ((t1, w1_out), (t2, w2_out)):
        for c in range(3):
            rows = src[4 * c : 4 * c + 4].reshape(CH, 384) * scale
            for a in range(3):
                for b in range(3):
                    at = (a * 4 + b) * CH
                    dst[9 * a + 3 * b + c] = rows[:, at : at + CH]
    for copy in copies:
        copy.wait()


def local(output_one, output_two, cotangent_one, cotangent_two, first_weight, second_weight, bricks):
    turned = pltpu.VMEM((B, B, CH, NX), BF)
    sums = pltpu.VMEM((CHUNKS, 8, 384), F32)
    hbm = pl.BlockSpec(memory_space=pl.ANY)
    vmem = pl.BlockSpec(memory_space=pltpu.VMEM)
    smem = pl.BlockSpec(memory_space=pltpu.SMEM)
    plain = pltpu.VMEM((CH, B, B, NX), BF)
    padded = pltpu.VMEM((B + 2, B + 2, CH, NX), BF)
    band = pltpu.VMEM((384, 512), BF)
    dma = pltpu.SemaphoreType.DMA
    r1, r2, g1, g2, t1, t2 = pl.pallas_call(
        fused,
        out_shape=(turned, turned, turned, turned, sums, sums),
        in_specs=[hbm, hbm, hbm, hbm, vmem, vmem, smem],
        out_specs=(vmem,) * 6,
        scratch_shapes=[plain] * 4
        + [padded, pltpu.VMEM((2, B + 2, B + 2, CH, NX), BF), padded]
        + [
            pltpu.VMEM((2, B, B, CH, NX), BF),
            pltpu.VMEM((256, 256), BF),
            band,
            band,
            band,
            band,
            pltpu.VMEM((384, 512), F32),
            pltpu.VMEM((2, CHUNKS, 8, 384), F32),
            pltpu.VMEM((2, ND, 8, 384), F32),
            pltpu.VMEM((2, NG, 8, 384), F32),
            pltpu.VMEM((2, CHUNKS, 8, 384), F32),
            dma((4,)),
            dma((3, 8)),
            dma((3, 8)),
            dma((2,)),
            dma((2,)),
            dma((2,)),
            dma((2,)),
            dma((2,)),
            dma((2,)),
        ],
        compiler_params=pltpu.CompilerParams(
            collective_id=0, has_side_effects=True, vmem_limit_bytes=51 * 1024 * 1024
        ),
        name="fused",
    )(output_one, output_two, cotangent_one, cotangent_two, first_weight, second_weight, bricks)

    scale = 1.0 / math.sqrt(float(B * ND * B * NG * NX))
    volume = jax.ShapeDtypeStruct((CH, B, B, NX), BF)
    weight = jax.ShapeDtypeStruct((27, CH, CH), F32)

    def back(*refs):
        natural(scale, *refs)

    return pl.pallas_call(
        back,
        out_shape=(volume, volume, volume, volume, weight, weight),
        in_specs=[vmem] * 6,
        out_specs=(hbm, hbm, hbm, hbm, vmem, vmem),
        scratch_shapes=[plain] * 4 + [pltpu.VMEM((256, 256), BF), dma((4, 2))],
        compiler_params=pltpu.CompilerParams(vmem_limit_bytes=20 * 1024 * 1024),
        name="natural",
    )(r1, r2, g1, g2, t1, t2)


def solution(mesh):
    slab = P(None, "depth", "group", None)
    return jax.shard_map(
        local,
        mesh=mesh,
        in_specs=(slab, slab, slab, slab, P(), P(), P("depth", None, None)),
        out_specs=(slab, slab, slab, slab, P(), P()),
        check_vma=False,
    )
```

```python
import math

import jax
import jax.numpy as jnp
from jax import lax
from jax.experimental import pallas as pl
from jax.experimental.pallas import tpu as pltpu
from jax.sharding import PartitionSpec as P

MESH = pl.DeviceIdType.MESH
BF = jnp.bfloat16
F32 = jnp.float32

CH = 32
B = 16
NX = 128
ND = 16
NG = 8
CHUNKS = 12
DIRS = ((0, -1), (0, 1), (-1, 0), (1, 0), (-1, -1), (-1, 1), (1, -1), (1, 1))
SIDES, ENDS, CORNERS = (0, 1), (2, 3), (4, 5, 6, 7)


def dot(a, b):
    return lax.dot_general(a, b, (((1,), (0,)), ((), ())), preferred_element_type=F32)


def dot_nt(a, b):
    return lax.dot_general(a, b, (((1,), (1,)), ((), ())), preferred_element_type=F32)


def permutation():
    row = lax.broadcasted_iota(jnp.int32, (256, 256), 0)
    col = lax.broadcasted_iota(jnp.int32, (256, 256), 1)
    return jnp.where((row & 15) * 16 + (row >> 4) == col, 1.0, 0.0).astype(BF)


def lane():
    return lax.broadcasted_iota(jnp.int32, (1, NX), 1)


def shift_up(values):
    return jnp.where(lane() == 0, 0.0, pltpu.roll(values, 1, 1))


def shift_down(values):
    return jnp.where(lane() == NX - 1, 0.0, pltpu.roll(values, NX - 1, 1))


def band_rows(blocks, out_ref):
    zeros = jnp.zeros((CH, NX), F32)
    for c in range(3):
        wide = jnp.concatenate([blocks(a, c) for a in range(3)] + [zeros], axis=1)
        for zo in range(2):
            for yo in range(2):
                turn = (zo * 4 + yo) * CH
                moved = wide if turn == 0 else pltpu.roll(wide, turn, 1)
                row = (c * 4 + zo * 2 + yo) * CH
                out_ref[row : row + CH, :] = moved.astype(BF)


def build_band(w_ref, out_ref):
    def blocks(a, c):
        taps = [w_ref[9 * a + 3 * b + c].astype(F32) for b in range(3)]
        return jnp.concatenate(taps + [jnp.zeros((CH, CH), F32)], axis=1)

    band_rows(blocks, out_ref)


def build_band_transposed(w_ref, out_ref):
    def blocks(a, c):
        taps = [w_ref[26 - (9 * a + 3 * b + c)].astype(F32) for b in range(3)]
        tall = jnp.concatenate(taps + [jnp.zeros((CH, CH), F32)], axis=0)
        square = jnp.concatenate([tall, jnp.zeros((NX, NX - CH), F32)], axis=1)
        return jnp.transpose(square)[:CH]

    band_rows(blocks, out_ref)


def fused(
    o1, o2, c1, c2, w1_ref, w2_ref, bricks_ref,
    q_o1, q_o2, q_c1, q_c2, t1_out, t2_out,
    n_o1, n_o2, n_c1, n_c2,
    p_u, p_pair, p_ef,
    shifted, perm, band_f, band_g, band_tf, band_tg, acc,
    part, rs_in, ar_in, tot,
    in_sem, hs, hr, rs_s, rs_r, ar_s, ar_r, ag_s, ag_r,
):
    depth = lax.axis_index("depth")
    group = lax.axis_index("group")

    def exists(dz, dy):
        ok = None
        for d, at, size in ((dz, depth, ND), (dy, group, NG)):
            if d == 0:
                continue
            here = at > 0 if d < 0 else at < size - 1
            ok = here if ok is None else jnp.logical_and(ok, here)
        return ok

    def clamp(dz, dy):
        return (
            jnp.clip(depth + dz, 0, ND - 1) if dz else depth,
            jnp.clip(group + dy, 0, NG - 1) if dy else group,
        )

    loads = [
        pltpu.make_async_copy(src, dst, in_sem.at[n])
        for n, (src, dst) in enumerate(((o1, n_o1), (c2, n_c2), (o2, n_o2), (c1, n_c1)))
    ]
    loads[0].start()

    barrier = pltpu.get_barrier_semaphore()

    def greet_depth(k, _):
        pl.semaphore_signal(
            barrier, inc=1, device_id=(lax.rem(depth + k, ND), group), device_id_type=MESH
        )
        return 0

    def greet_group(k, _):
        pl.semaphore_signal(
            barrier, inc=1, device_id=(depth, lax.rem(group + k, NG)), device_id_type=MESH
        )
        return 0

    lax.fori_loop(1, ND, greet_depth, 0, unroll=ND - 1)
    lax.fori_loop(1, NG, greet_group, 0, unroll=NG - 1)
    for dz, dy in DIRS:
        if dz != 0 and dy != 0:

            @pl.when(exists(dz, dy))
            def _():
                pl.semaphore_signal(barrier, inc=1, device_id=clamp(dz, dy), device_id_type=MESH)

    perm[...] = permutation()
    place = lane() >> 4
    mask = jnp.zeros((1, NX), F32)
    for slot in range(8):
        mask = jnp.where(place == bricks_ref[0, group, slot], 1.0, mask)

    p_l, p_eg = p_pair.at[0], p_pair.at[1]
    volumes = (p_u, p_pair, p_ef)

    def zero_plane(ref, z):
        def body(y, _):
            ref[z, y] = jnp.zeros((CH, NX), BF)
            return 0

        lax.fori_loop(0, B + 2, body, 0)

    def zero_row(ref, y):
        def body(z, _):
            ref[z, y] = jnp.zeros((CH, NX), BF)
            return 0

        lax.fori_loop(0, B + 2, body, 0)

    for d, at in ((depth == 0, 0), (depth == ND - 1, B + 1)):

        @pl.when(d)
        def _():
            for ref in (p_u, p_l, p_eg, p_ef):
                zero_plane(ref, at)

    for d, at in ((group == 0, 0), (group == NG - 1, B + 1)):

        @pl.when(d)
        def _():
            for ref in (p_u, p_l, p_eg, p_ef):
                zero_row(ref, at)

    def relayout(src, dst, masked=None):
        def body(k, _):
            for h in range(2):
                pair = jnp.concatenate(
                    [src[pl.ds(16 * h, 16), 2 * k + zz].reshape(256, NX) for zz in range(2)], axis=1
                )
                turned = dot(perm[...], pair)
                for zz in range(2):
                    half = turned[:, NX * zz : NX * (zz + 1)]
                    dst[2 * k + zz, :, 16 * h : 16 * h + 16, :] = half.astype(BF).reshape(16, 16, NX)
                    if masked is not None:
                        masked[2 * k + 1 + zz, 1 : B + 1, 16 * h : 16 * h + 16, :] = (
                            (half * mask).astype(BF).reshape(16, 16, NX)
                        )
            return 0

        lax.fori_loop(0, 8, body, 0, unroll=8)

    def side(d, sending):
        if d == 0:
            return pl.ds(1, B)
        if sending:
            return pl.ds(B if d > 0 else 1, 1)
        return pl.ds(0 if d > 0 else B + 1, 1)

    def halo(number, k):
        dz, dy = DIRS[k]
        ref = volumes[number]
        both = (pl.ds(0, 2),) if number == 1 else ()
        return pltpu.make_async_remote_copy(
            src_ref=ref.at[*both, side(dz, True), side(dy, True)],
            dst_ref=ref.at[*both, side(dz, False), side(dy, False)],
            send_sem=hs.at[number, k],
            recv_sem=hr.at[number, k],
            device_id=clamp(dz, dy),
            device_id_type=MESH,
        )

    def halo_start(number):
        for k, (dz, dy) in enumerate(DIRS):

            @pl.when(exists(dz, dy))
            def _():
                halo(number, k).start()

    def halo_arrived(number, which):
        for k in which:
            dz, dy = DIRS[k]

            @pl.when(exists(-dz, -dy))
            def _():
                halo(number, k).wait_recv()

    def halo_sent(number):
        for k, (dz, dy) in enumerate(DIRS):

            @pl.when(exists(dz, dy))
            def _():
                halo(number, k).wait_send()

    def windows(ref, i, pair):
        return jnp.concatenate(
            [ref[pl.ds(2 * i, 4), pl.ds(2 * j, 4)].reshape(512, NX) for j in pair], axis=1
        )

    def join(product, r):
        cut = product[:, NX * r : NX * (r + 1)]
        return cut[128:256] + shift_up(cut[0:128]) + shift_down(cut[256:384])

    def get(ref, i, j):
        return ref[pl.ds(2 * i, 2), pl.ds(2 * j, 2)].reshape(128, NX).astype(F32)

    def put(ref, i, j, values):
        ref[pl.ds(2 * i, 2), pl.ds(2 * j, 2)] = values.reshape(2, 2, CH, NX)

    def put_inner(ref, i, j, values):
        ref[pl.ds(2 * i + 1, 2), pl.ds(2 * j + 1, 2)] = values.reshape(2, 2, CH, NX)

    def put_shifted(i, j, errors):
        wide = errors.astype(F32)
        for number, moved in enumerate((shift_down(wide), shift_up(wide))):
            shifted[number, pl.ds(2 * i, 2), pl.ds(2 * j, 2)] = moved.astype(BF).reshape(2, 2, CH, NX)

    def inner_patches(body):
        def step(i, _):
            for j in (1, 3, 5):
                body(i, (j, j + 1))
            return 0

        lax.fori_loop(1, 7, step, 0, unroll=6)

    def outer_patches(body, number):
        def end(n, _):
            j = 2 * lax.rem(n, 3) + 1
            body(7 * lax.div(n, 3), (j, j + 1))
            return 0

        def edge(i, _):
            body(i, (0, 7))
            return 0

        halo_arrived(number, ENDS)
        lax.fori_loop(0, 6, end, 0, unroll=6)
        halo_arrived(number, SIDES)
        lax.fori_loop(1, 7, edge, 0, unroll=6)
        halo_arrived(number, CORNERS)
        body(0, (0, 7))
        body(7, (0, 7))

    def sigmoid(v):
        return 0.5 + 0.5 * jnp.tanh(0.5 * v)

    def weight_gradient(w, errors_ref, source_ref):
        acc[...] = jnp.zeros_like(acc)

        def body(i, _):
            left, right = [], []
            for j in range(8):
                low = shifted[0, pl.ds(2 * i, 2), 2 * j : 2 * j + 2].reshape(128, NX)
                mid = errors_ref[pl.ds(2 * i + 1, 2), 2 * j + 1 : 2 * j + 3].reshape(128, NX)
                top = shifted[1, pl.ds(2 * i, 2), 2 * j : 2 * j + 2].reshape(128, NX)
                left.append(jnp.concatenate([low, mid, top], axis=0))
                right.append(source_ref[pl.ds(2 * i, 4), 2 * j : 2 * j + 4].reshape(512, NX))
            acc[...] += dot_nt(jnp.concatenate(left, axis=1), jnp.concatenate(right, axis=1))
            return 0

        lax.fori_loop(0, 8, body, 0, unroll=4)
        for c in range(3):
            total = None
            for zo in range(2):
                for yo in range(2):
                    row = (c * 4 + zo * 2 + yo) * CH
                    turn = (zo * 4 + yo) * CH
                    rows = acc[row : row + CH, :]
                    if turn:
                        rows = pltpu.roll(rows, 512 - turn, 1)
                    total = rows if total is None else total + rows
            part[w, 4 * c : 4 * c + 4] = total[:, :384].reshape(4, 8, 384)

    own = lax.rem(depth, CHUNKS)
    owner = depth < CHUNKS

    def rs_copy(w, k):
        peer = lax.rem(depth + k, ND)
        return pltpu.make_async_remote_copy(
            src_ref=part.at[w, lax.rem(peer, CHUNKS)],
            dst_ref=rs_in.at[w, depth],
            send_sem=rs_s.at[w],
            recv_sem=rs_r.at[w],
            device_id=(peer, group),
            device_id_type=MESH,
        )

    def ar_copy(w, k):
        return pltpu.make_async_remote_copy(
            src_ref=ar_in.at[w, group],
            dst_ref=ar_in.at[w, group],
            send_sem=ar_s.at[w],
            recv_sem=ar_r.at[w],
            device_id=(depth, lax.rem(group + k, NG)),
            device_id_type=MESH,
        )

    def ag_copy(w, k):
        return pltpu.make_async_remote_copy(
            src_ref=tot.at[w, own],
            dst_ref=tot.at[w, own],
            send_sem=ag_s.at[w],
            recv_sem=ag_r.at[w],
            device_id=(lax.rem(depth + k, ND), group),
            device_id_type=MESH,
        )

    def await_chunks(sem, w, count):
        ref = rs_in.at[w, pl.ds(0, count)]
        pltpu.make_async_copy(ref, ref, sem.at[w]).wait()

    def each_peer(size, act, only_owners=False):
        def body(k, _):
            if only_owners:

                @pl.when(lax.rem(depth + k, ND) < CHUNKS)
                def _():
                    act(k)
            else:
                act(k)
            return 0

        lax.fori_loop(1, size, body, 0, unroll=size - 1)

    def reduce_start(w):
        each_peer(ND, lambda k: rs_copy(w, k).start(), True)

    def reduce_middle(w):
        @pl.when(owner)
        def _():
            rs_in[w, depth] = part[w, own]
            await_chunks(rs_r, w, ND - 1)
            ar_in[w, group] = jnp.sum(rs_in[w], axis=0)
            each_peer(NG, lambda k: ar_copy(w, k).start())

    def reduce_spread(w):
        @pl.when(owner)
        def _():
            await_chunks(ar_r, w, NG - 1)
            tot[w, own] = jnp.sum(ar_in[w], axis=0)
            each_peer(ND, lambda k: ag_copy(w, k).start())

    def reduce_end(w):
        @pl.when(owner)
        def _():
            await_chunks(ag_r, w, CHUNKS - 1)
            await_chunks(rs_s, w, CHUNKS - 1)
            await_chunks(ar_s, w, NG - 1)
            await_chunks(ag_s, w, ND - 1)

        @pl.when(jnp.logical_not(owner))
        def _():
            await_chunks(ag_r, w, CHUNKS)
            await_chunks(rs_s, w, CHUNKS)

    build_band(w2_ref, band_g)
    loads[0].wait()
    for load in loads[1:]:
        load.start()
    relayout(n_o1, q_o1, p_u)
    near = jnp.minimum(depth, 1) + jnp.minimum(ND - 1 - depth, 1)
    aside = jnp.minimum(group, 1) + jnp.minimum(NG - 1 - group, 1)
    pl.semaphore_wait(barrier, ND - 1 + NG - 1 + near * aside)
    halo_start(0)
    loads[1].wait()
    relayout(n_c2, q_c2)
    loads[2].wait()
    relayout(n_o2, q_o2)
    loads[3].wait()
    relayout(n_c1, q_c1)
    build_band(w1_ref, band_f)
    build_band_transposed(w1_ref, band_tf)
    build_band_transposed(w2_ref, band_tg)

    def first(i, pair):
        product = dot(band_g[...], windows(p_u, i, pair))
        for r, j in enumerate(pair):
            v = join(product, r)
            s = sigmoid(v)
            silu = v * s
            shaped = (mask * silu).astype(BF).astype(F32)
            slope = s + silu * (1.0 - s)
            errors = (mask * get(q_c2, i, j) * slope).astype(BF)
            restored = (get(q_o2, i, j) - shaped).astype(BF)
            put(q_o2, i, j, restored)
            put_inner(p_l, i, j, (restored.astype(F32) * mask).astype(BF))
            put_inner(p_eg, i, j, errors)
            put_shifted(i, j, errors)

    inner_patches(first)
    outer_patches(first, 0)
    halo_start(1)
    weight_gradient(0, p_eg, p_u)
    reduce_start(0)

    def second(i, pair):
        spread = dot(band_tg[...], windows(p_eg, i, pair))
        product = dot(band_f[...], windows(p_l, i, pair))
        for r, j in enumerate(pair):
            total = (get(q_c1, i, j) + mask * join(spread, r)).astype(BF)
            put(q_c1, i, j, total)
            v = join(product, r)
            s = sigmoid(v)
            silu = v * s
            shaped = (mask * silu).astype(BF).astype(F32)
            slope = s + silu * (1.0 - s)
            errors = (mask * total.astype(F32) * slope).astype(BF)
            put(q_o1, i, j, (get(q_o1, i, j) - shaped).astype(BF))
            put_inner(p_ef, i, j, errors)
            put_shifted(i, j, errors)

    inner_patches(second)
    outer_patches(second, 1)
    halo_start(2)
    reduce_middle(0)
    weight_gradient(1, p_ef, p_l)
    reduce_start(1)

    def third(i, pair):
        spread = dot(band_tf[...], windows(p_ef, i, pair))
        for r, j in enumerate(pair):
            put(q_c2, i, j, (get(q_c2, i, j) + mask * join(spread, r)).astype(BF))

    inner_patches(third)
    reduce_spread(0)
    reduce_middle(1)
    outer_patches(third, 2)
    reduce_spread(1)
    reduce_end(0)
    reduce_end(1)
    for number in range(3):
        halo_sent(number)
    t2_out[...] = tot[0]
    t1_out[...] = tot[1]


def natural(
    scale, r1, r2, g1, g2, t1, t2,
    r1_out, r2_out, g1_out, g2_out, w1_out, w2_out,
    n1, n2, n3, n4, perm, sems,
):
    perm[...] = permutation()
    copies = []
    for number, (src, wide, out) in enumerate(
        ((r1, n1, r1_out), (r2, n2, r2_out), (g1, n3, g1_out), (g2, n4, g2_out))
    ):
        for h in range(2):

            def body(k, _):
                pair = jnp.concatenate(
                    [src[2 * k + zz, :, 16 * h : 16 * h + 16, :].reshape(256, NX) for zz in range(2)],
                    axis=1,
                )
                turned = dot(perm[...], pair)
                for zz in range(2):
                    half = turned[:, NX * zz : NX * (zz + 1)]
                    wide[16 * h : 16 * h + 16, 2 * k + zz] = half.astype(BF).reshape(16, 16, NX)
                return 0

            lax.fori_loop(0, 8, body, 0, unroll=8)
            copy = pltpu.make_async_copy(
                wide.at[pl.ds(16 * h, 16)], out.at[pl.ds(16 * h, 16)], sems.at[number, h]
            )
            copy.start()
            copies.append(copy)
    for src, dst in ((t1, w1_out), (t2, w2_out)):
        for c in range(3):
            rows = src[4 * c : 4 * c + 4].reshape(CH, 384) * scale
            for a in range(3):
                for b in range(3):
                    at = (a * 4 + b) * CH
                    dst[9 * a + 3 * b + c] = rows[:, at : at + CH]
    for copy in copies:
        copy.wait()


def local(output_one, output_two, cotangent_one, cotangent_two, first_weight, second_weight, bricks):
    turned = pltpu.VMEM((B, B, CH, NX), BF)
    sums = pltpu.VMEM((CHUNKS, 8, 384), F32)
    hbm = pl.BlockSpec(memory_space=pl.ANY)
    vmem = pl.BlockSpec(memory_space=pltpu.VMEM)
    smem = pl.BlockSpec(memory_space=pltpu.SMEM)
    plain = pltpu.VMEM((CH, B, B, NX), BF)
    padded = pltpu.VMEM((B + 2, B + 2, CH, NX), BF)
    band = pltpu.VMEM((384, 512), BF)
    dma = pltpu.SemaphoreType.DMA
    r1, r2, g1, g2, t1, t2 = pl.pallas_call(
        fused,
        out_shape=(turned, turned, turned, turned, sums, sums),
        in_specs=[hbm, hbm, hbm, hbm, vmem, vmem, smem],
        out_specs=(vmem,) * 6,
        scratch_shapes=[plain] * 4
        + [padded, pltpu.VMEM((2, B + 2, B + 2, CH, NX), BF), padded]
        + [
            pltpu.VMEM((2, B, B, CH, NX), BF),
            pltpu.VMEM((256, 256), BF),
            band,
            band,
            band,
            band,
            pltpu.VMEM((384, 512), F32),
            pltpu.VMEM((2, CHUNKS, 8, 384), F32),
            pltpu.VMEM((2, ND, 8, 384), F32),
            pltpu.VMEM((2, NG, 8, 384), F32),
            pltpu.VMEM((2, CHUNKS, 8, 384), F32),
            dma((4,)),
            dma((3, 8)),
            dma((3, 8)),
            dma((2,)),
            dma((2,)),
            dma((2,)),
            dma((2,)),
            dma((2,)),
            dma((2,)),
        ],
        compiler_params=pltpu.CompilerParams(
            collective_id=0, has_side_effects=True, vmem_limit_bytes=51 * 1024 * 1024
        ),
        name="fused",
    )(output_one, output_two, cotangent_one, cotangent_two, first_weight, second_weight, bricks)

    scale = 1.0 / math.sqrt(float(B * ND * B * NG * NX))
    volume = jax.ShapeDtypeStruct((CH, B, B, NX), BF)
    weight = jax.ShapeDtypeStruct((27, CH, CH), F32)

    def back(*refs):
        natural(scale, *refs)

    return pl.pallas_call(
        back,
        out_shape=(volume, volume, volume, volume, weight, weight),
        in_specs=[vmem] * 6,
        out_specs=(hbm, hbm, hbm, hbm, vmem, vmem),
        scratch_shapes=[plain] * 4 + [pltpu.VMEM((256, 256), BF), dma((4, 2))],
        compiler_params=pltpu.CompilerParams(vmem_limit_bytes=20 * 1024 * 1024),
        name="natural",
    )(r1, r2, g1, g2, t1, t2)


def solution(mesh):
    slab = P(None, "depth", "group", None)
    return jax.shard_map(
        local,
        mesh=mesh,
        in_specs=(slab, slab, slab, slab, P(), P(), P("depth", None, None)),
        out_specs=(slab, slab, slab, slab, P(), P()),
        check_vma=False,
    )
```
